1024 devices in a mesh: dp: 8 (over y), group: 8 (over x), node: 16 (over z, core).
Axes of the slice: x: 8, y: 8, z: 8, core: 2. Of those that a mesh axis runs over, the one named last changes fastest.
Arguments:
- tokens: bfloat16 [16384, 2048], P(('dp', 'group', 'node')), may hold values from -6 to 6
- cotangent: bfloat16 [16384, 2048], P(('dp', 'group', 'node')), may hold values from -6 to 6
- expert_ids: int32 [16384, 8], P(('dp', 'group', 'node')), may hold values from 0 to 127, as said below
- node_groups: int32 [16384, 4], P(('dp', 'group', 'node')), may hold values from 0 to 7, as said below
- gate_weight: bfloat16 [16384, 8], P(('dp', 'group', 'node')), may hold values from 0.019897461 to 0.29882812
- gate_proj: bfloat16 [128, 2048, 384], P(('group', 'node')), may hold values from -0.125 to 0.125
- up_proj: bfloat16 [128, 2048, 384], P(('group', 'node')), may hold values from -0.125 to 0.125
- down_proj: bfloat16 [128, 384, 2048], P(('group', 'node')), may hold values from -0.3125 to 0.3125
Outputs:
- grad_tokens: bfloat16 [16384, 2048], P(('dp', 'group', 'node'))
- grad_gate_proj: bfloat16 [128, 2048, 384], P(('group', 'node'), 'dp')
- grad_up_proj: bfloat16 [128, 2048, 384], P(('group', 'node'), 'dp')
- grad_down_proj: bfloat16 [128, 384, 2048], P(('group', 'node'), None, 'dp')
The draws below stay inside these ranges and needn't reach their ends.
Inputs may be any that keep to these rules, and one draw needn't show every extreme that they name: `expert_ids`: each token names 8 distinct experts, 2 of them in each of 4 distinct node groups. Among the tokens of all devices that share a dp index and a node index, no expert is named more than 16 times, and in every such set some expert is named exactly 16 times. `node_groups`: entries of a token's row may repeat; every listed group holds some of the token's named experts, and a named expert outside the listed groups carries no route.
All inputs are finite; a program needn't handle non-finite values.
Results may differ from the reference program's by a relative error of at most 0.017.
Values may be sent and summed in bfloat16 or wider, within the bound.
No kernel may reach another device: no remote copies, remote signals or barrier semaphores. Data moves between devices by JAX's collectives and lax.ppermute only.
A program may use at most 64 MiB of HBM per device.

```python
import jax
import jax.numpy as jnp
from jax import lax

D = 2048
HID = 384
TOPK = 8
TOK_DEV = 16
GROUP_LIMIT = 4
EXPERTS = 128
TOKENS = 16384
CAPACITY = 16
N_DP = 8
N_GROUP = 8
N_NODE = 16


def route_plan(key):
    family = N_GROUP * TOK_DEV
    per_group = TOPK // GROUP_LIMIT
    keys = jax.random.split(key, 4)
    noise = jax.random.randint(keys[0], (N_DP, N_NODE, family, N_GROUP), 0, 1 << 20)
    favour = jax.random.randint(keys[1], (N_DP, 1, 1, N_GROUP), 0, 1 << 20)
    forced = jax.random.randint(keys[2], (N_DP, N_NODE, 1, 1), 0, N_GROUP)
    needed = N_NODE * (CAPACITY - 1) // per_group + 1
    position = jnp.arange(family, dtype=jnp.int32)[None, None, :, None]
    group_index = jnp.arange(N_GROUP, dtype=jnp.int32)
    boost = jnp.where((group_index == forced) & (position < needed), 1 << 22, 0)
    scores = (noise + favour + boost) * N_GROUP + group_index
    _, chosen = lax.top_k(scores, GROUP_LIMIT)
    chosen = chosen.astype(jnp.int32)
    picked = jnp.any(chosen[..., None] == group_index, axis=-2).astype(jnp.int32)
    ranks = jnp.cumsum(picked, axis=2) - picked
    chosen_rank = jnp.take_along_axis(ranks, chosen, axis=3)
    slot_of = (per_group * chosen_rank[..., None] + jnp.arange(per_group, dtype=jnp.int32)) % N_NODE
    order_scores = jax.random.randint(keys[3], (N_DP, N_NODE, N_GROUP, N_NODE), 0, 1 << 20) * N_NODE + jnp.arange(N_NODE, dtype=jnp.int32)
    shuffled = jnp.argsort(order_scores, axis=-1).astype(jnp.int32).reshape(N_DP, N_NODE, N_GROUP * N_NODE)
    flat_index = (chosen[..., None] * N_NODE + slot_of).reshape(N_DP, N_NODE, family * TOPK)
    node_of = jnp.take_along_axis(shuffled, flat_index, axis=2).reshape(N_DP, N_NODE, family, GROUP_LIMIT, per_group)
    expert_of = chosen[..., None] * N_NODE + node_of
    expert_of = expert_of.reshape(N_DP, N_NODE, N_GROUP, TOK_DEV, TOPK)
    expert_of = jnp.transpose(expert_of, (0, 2, 1, 3, 4)).reshape(TOKENS, TOPK)
    groups_of = chosen.reshape(N_DP, N_NODE, N_GROUP, TOK_DEV, GROUP_LIMIT)
    groups_of = jnp.transpose(groups_of, (0, 2, 1, 3, 4)).reshape(TOKENS, GROUP_LIMIT)
    return (expert_of.astype(jnp.int32), groups_of.astype(jnp.int32))


def draw_expert_ids(key, part):
    planned = route_plan(key)
    return planned[0]


def draw_node_groups(key, part):
    planned = route_plan(key)
    key = jax.random.fold_in(key, 12)
    groups = planned[1]
    keys = jax.random.split(key, 2)
    flagged = jax.random.randint(keys[0], (TOKENS, 1), 0, 2)
    dropped = jax.random.randint(keys[1], (TOKENS, 1), 0, GROUP_LIMIT).astype(jnp.int32)
    column = jnp.arange(GROUP_LIMIT, dtype=jnp.int32)[None, :]
    other = jnp.take_along_axis(groups, (dropped + 1) % GROUP_LIMIT, axis=1)
    replaced = jnp.where((column == dropped) & (flagged == 1), other, groups)
    return replaced.astype(jnp.int32)


def levels(stream_key, extent, shards, low, largest):
    gain, own = 1.0, jax.random.fold_in(stream_key, 6)
    for dim, shards_of in shards:
        steps = jnp.exp(jax.random.uniform(jax.random.fold_in(own, dim), (shards_of,), jnp.float32, low / len(shards), largest / len(shards)))
        gain = gain * jnp.repeat(steps, extent[dim] // shards_of).reshape([-1 if axis == dim else 1 for axis in range(len(extent))])
    return gain


def bell_draw(rng, dims, deviation, bound, cuts=(), kind=jnp.bfloat16):
    values = deviation * jax.random.normal(rng, dims, jnp.float32)
    if cuts:
        values = values * levels(rng, dims, cuts, -0.22, 0.18)
    return jnp.clip(values, -bound, bound).astype(kind)


def setup_inputs(seed: int = 0) -> dict:
    seeds = jax.random.split(jax.random.key(seed), 9)
    return {
        "tokens": bell_draw(seeds[0], (TOKENS, D), 1.0, 6.0, ((0, 1024),)),
        "cotangent": bell_draw(seeds[1], (TOKENS, D), 1.0, 6.0, ((0, 1024),)),
        "expert_ids": draw_expert_ids(jax.random.fold_in(seeds[8], 71), 0),
        "node_groups": draw_node_groups(jax.random.fold_in(seeds[8], 71), 0),
        "gate_weight": jnp.clip(0.019897461 + 0.27893066 * jax.random.uniform(seeds[4], (TOKENS, TOPK), jnp.float32) ** levels(seeds[4], (TOKENS, TOPK), ((0, 1024),), -0.2, 0.2), 0.019897461, 0.29882812).astype(jnp.bfloat16),
        "gate_proj": bell_draw(seeds[5], (EXPERTS, D, HID), D ** -0.5, 0.125, ((0, 128),)),
        "up_proj": bell_draw(seeds[6], (EXPERTS, D, HID), D ** -0.5, 0.125, ((0, 128),)),
        "down_proj": bell_draw(seeds[7], (EXPERTS, HID, D), HID ** -0.5, 0.3125, ((0, 128),)),
    }


def expert_pass(routed_rows, cot_rows, gate_matrix, up_matrix, down_matrix):
    contract = (((1,), (1,)), ((), ()))
    gate_value = jnp.dot(routed_rows, gate_matrix, preferred_element_type=jnp.float32)
    up_value = jnp.dot(routed_rows, up_matrix, preferred_element_type=jnp.float32)
    sigmoid_gate = jax.nn.sigmoid(gate_value)
    activated = gate_value * sigmoid_gate
    hidden = (activated * up_value).astype(jnp.bfloat16)
    hidden_grad = lax.dot_general(cot_rows, down_matrix, contract, preferred_element_type=jnp.float32)
    gate_grad = (hidden_grad * up_value * sigmoid_gate * (1.0 + gate_value * (1.0 - sigmoid_gate))).astype(jnp.bfloat16)
    up_grad = (hidden_grad * activated).astype(jnp.bfloat16)
    route_grad = lax.dot_general(gate_grad, gate_matrix, contract, preferred_element_type=jnp.float32)
    route_grad = route_grad + lax.dot_general(up_grad, up_matrix, contract, preferred_element_type=jnp.float32)
    return hidden, gate_grad, up_grad, route_grad.astype(jnp.bfloat16)


def over_rows(left, right):
    return lax.dot_general(left, right, (((0,), (0,)), ((), ())), preferred_element_type=jnp.float32)


def rounded(value):
    return lax.optimization_barrier(value.astype(jnp.bfloat16)).astype(jnp.float32)


def reference(tokens, cotangent, expert_ids, node_groups, gate_weight, gate_proj, up_proj, down_proj):
    per_data = TOKENS // N_DP
    most_rows = N_NODE * CAPACITY
    token_iota = jnp.arange(per_data, dtype=jnp.int32)
    gate_values = gate_weight.astype(jnp.float32)

    def expert_step(carry, expert_index):
        total, group_sum = carry
        group_index = expert_index // N_NODE
        hits = expert_ids == expert_index
        routed = jnp.any(hits, axis=1) & jnp.any(node_groups == group_index, axis=1)
        weight_of = jnp.sum(jnp.where(hits, gate_values, jnp.float32(0.0)), axis=1)
        weight_of = jnp.where(routed, weight_of, jnp.float32(0.0))
        gate_matrix = gate_proj[expert_index]
        up_matrix = up_proj[expert_index]
        down_matrix = down_proj[expert_index]

        def data_step(inner, data_index):
            group_acc, sum_gate, sum_up, sum_down = inner
            start = (data_index * per_data).astype(jnp.int32)
            local_routed = lax.dynamic_slice_in_dim(routed, start, per_data)
            order_key = jnp.where(local_routed, token_iota, token_iota + per_data)
            chosen = jnp.argsort(order_key)[:most_rows].astype(jnp.int32) + start
            chosen_routed = routed[chosen]
            chosen_weight = weight_of[chosen]
            routed_rows = jnp.where(chosen_routed[:, None], tokens[chosen], jnp.zeros((), tokens.dtype))
            cot_rows = (chosen_weight[:, None] * cotangent[chosen].astype(jnp.float32)).astype(jnp.bfloat16)
            hidden, gate_grad, up_grad, route_grad = expert_pass(routed_rows, cot_rows, gate_matrix, up_matrix, down_matrix)
            sum_gate = sum_gate + rounded(over_rows(routed_rows, gate_grad))
            sum_up = sum_up + rounded(over_rows(routed_rows, up_grad))
            sum_down = sum_down + rounded(over_rows(hidden, cot_rows))
            group_acc = group_acc.at[chosen].add(route_grad.astype(jnp.float32))
            return (group_acc, sum_gate, sum_up, sum_down), None

        start_sums = (group_sum, jnp.zeros((D, HID), jnp.float32), jnp.zeros((D, HID), jnp.float32), jnp.zeros((HID, D), jnp.float32))
        (group_sum, sum_gate, sum_up, sum_down), _ = lax.scan(data_step, start_sums, jnp.arange(N_DP, dtype=jnp.int32))
        closing = (expert_index % N_NODE) == N_NODE - 1
        total = jnp.where(closing, total + rounded(group_sum), total)
        group_sum = jnp.where(closing, jnp.zeros_like(group_sum), group_sum)
        return (total, group_sum), (sum_gate.astype(jnp.bfloat16), sum_up.astype(jnp.bfloat16), sum_down.astype(jnp.bfloat16))

    start_carry = (jnp.zeros((TOKENS, D), jnp.float32), jnp.zeros((TOKENS, D), jnp.float32))
    (total, _), grads = lax.scan(expert_step, start_carry, jnp.arange(EXPERTS, dtype=jnp.int32))
    return total.astype(jnp.bfloat16), grads[0], grads[1], grads[2]
```

```python
import functools

import jax
import jax.numpy as jnp
from jax import lax
from jax.experimental import pallas as pl
from jax.experimental.pallas import tpu as pltpu
from jax.sharding import PartitionSpec as P

F32 = jnp.float32
BF16 = jnp.bfloat16
LANES = 128


def contract(left, right, left_dim, right_dim):
    return lax.dot_general(
        left, right, (((left_dim,), (right_dim,)), ((), ())), preferred_element_type=F32
    )


def add(left, right):
    return (left.astype(F32) + right.astype(F32)).astype(BF16)


def to_owners(partial, returned, send_home):
    count, rows, _ = partial.shape
    nodes = lax.axis_size("node")
    half, reach = rows // 2, count // 2
    me = lax.axis_index("dp")
    first = jnp.where((me + lax.axis_index("node")) % 2 == 0, 1, -1)

    def exchange(block, flip):
        pairs = []
        for i in range(count):
            for n in range(nodes):
                step = 1 if (i + n + flip) % 2 == 0 else -1
                pairs.append((i * nodes + n, (i + step) % count * nodes + n))
        return lax.ppermute(block, ("dp", "node"), pairs)

    def own(offset):
        return lax.dynamic_index_in_dim(partial, (me + offset + count) % count, 0, keepdims=False)

    farthest = own(reach)
    turn, home = 0, None
    arrived = [exchange(farthest[:half], 0), exchange(farthest[half:], 1)]
    for hop in range(reach - 1, 0, -1):
        turn = 1 - turn
        toward = first if turn == 0 else -first
        blocks = [own(toward * hop), own(-toward * hop)]
        if hop == reach - 1:
            blocks = [
                jnp.concatenate([add(blocks[0][:half], arrived[0]), blocks[0][half:]], axis=0),
                jnp.concatenate([blocks[1][:half], add(blocks[1][half:], arrived[1])], axis=0),
            ]
        else:
            blocks = [add(mine, sent) for mine, sent in zip(blocks, arrived)]
        if hop == reach - 2:
            blocks, returned = lax.optimization_barrier((blocks, returned))
            home = send_home(returned)
        if hop == reach - 3:
            blocks, home = lax.optimization_barrier((blocks, home))
        arrived = [exchange(blocks[0], turn), exchange(blocks[1], 1 - turn)]
    total = own(0).astype(F32) + arrived[0].astype(F32) + arrived[1].astype(F32)
    return total.astype(BF16), home


def send_kernel(node_count, tokens, cotangent, expert_ids, node_groups, gate_weight, sent):
    group_count, tok_count, _ = sent.shape
    width = tokens.shape[1]
    choices, limit = expert_ids.shape[0], node_groups.shape[0]
    weights = gate_weight[...].astype(F32)
    expert = lax.broadcasted_iota(jnp.int32, (group_count * node_count, tok_count), 0)
    table = jnp.zeros(expert.shape, F32)
    for k in range(choices):
        table = table + jnp.where(expert_ids[k : k + 1, :] == expert, weights[k : k + 1, :], 0.0)
    for g in range(group_count):
        picked = node_groups[0:1, :] == g
        for j in range(1, limit):
            picked = picked | (node_groups[j : j + 1, :] == g)
        block = jnp.where(picked, table[g * node_count : (g + 1) * node_count, :], 0.0)
        sent[g, :, :width] = tokens[...]
        sent[g, :, width : 2 * width] = cotangent[...]
        sent[g, :, 2 * width :] = jnp.zeros((tok_count, LANES), BF16)
        sent[g, :node_count, 2 * width : 2 * width + tok_count] = block.astype(BF16)


def slot_kernel(arrived, slots, select):
    group_count, tok_count, _ = arrived.shape
    node_count, capacity, width = slots.shape
    width = width // 2
    family = group_count * tok_count
    table = [arrived[g, :node_count, 2 * width : 2 * width + tok_count] for g in range(group_count)]
    table = jnp.concatenate([part.astype(F32) for part in table], axis=1)
    routed = table > 0
    row = lax.broadcasted_iota(jnp.int32, (family, family), 0)
    column = lax.broadcasted_iota(jnp.int32, (family, family), 1)
    earlier = jnp.where(row < column, 1.0, 0.0).astype(BF16)
    position = contract(jnp.where(routed, 1.0, 0.0).astype(BF16), earlier, 1, 0)
    place = jnp.where(routed, position, -1.0)[:, None, :]
    slot = lax.broadcasted_iota(jnp.int32, (node_count, capacity, family), 1).astype(F32)
    taken = place == slot
    picks = jnp.where(taken, 1.0, 0.0).reshape(node_count * capacity, family).astype(BF16)
    weighted = jnp.where(taken, table[:, None, :], 0.0).reshape(node_count * capacity, family).astype(BF16)
    select[...] = picks
    cut = width // 4
    for start in range(0, 2 * width, cut):
        part = slice(start, start + cut)
        block = arrived[:, :, part].reshape(family, cut)
        out = contract(picks if start < width else weighted, block, 1, 0)
        slots[:, :, part] = out.reshape(node_count, capacity, cut).astype(BF16)


def expert_kernel(
    landed, gate_hbm, up_hbm, down_hbm, hidden, pair_grad, route_grad, gate_proj, up_proj, down_proj, done
):
    width, hid = gate_proj.shape
    loads = [
        pltpu.make_async_copy(gate_hbm, gate_proj, done.at[0]),
        pltpu.make_async_copy(up_hbm, up_proj, done.at[1]),
        pltpu.make_async_copy(down_hbm, down_proj, done.at[2]),
    ]
    for load in loads:
        load.start()
    loads[0].wait()
    gate_value = contract(landed[:, :width], gate_proj[...], 1, 0)
    loads[1].wait()
    up_value = contract(landed[:, :width], up_proj[...], 1, 0)
    sigmoid = 1.0 / (1.0 + jnp.exp(-gate_value))
    silu = gate_value * sigmoid
    hidden[...] = (silu * up_value).astype(BF16)
    loads[2].wait()
    hidden_grad = contract(landed[:, width:], down_proj[...], 1, 1)
    slope = up_value * sigmoid * (1.0 + gate_value * (1.0 - sigmoid))
    pair_grad[:, :hid] = (hidden_grad * slope).astype(BF16)
    pair_grad[:, hid:] = (hidden_grad * silu).astype(BF16)
    cut = width // 4
    for start in range(0, width, cut):
        part = slice(start, start + cut)
        grad = contract(pair_grad[:, :hid], gate_proj[part, :], 1, 1)
        grad = grad + contract(pair_grad[:, hid:], up_proj[part, :], 1, 1)
        route_grad[:, part] = grad.astype(BF16)


def weights_kernel(landed, pair_grad, hidden, partial):
    count, cut, _ = partial.shape
    pair = pair_grad.shape[1]
    width = count * cut
    for block in range(count):
        rows = landed[:, block * cut : (block + 1) * cut]
        cot_rows = landed[:, width + block * cut : width + (block + 1) * cut]
        partial[block, :, :pair] = contract(rows, pair_grad[...], 0, 0).astype(BF16)
        partial[block, :, pair:] = contract(cot_rows, hidden[...], 0, 0).astype(BF16)


def run(kernel, out, *args, flops=0, **kwargs):
    held = sum(x.size * x.dtype.itemsize for x in (*args, *out))
    return pl.pallas_call(
        kernel,
        out_shape=out,
        cost_estimate=pl.CostEstimate(flops=flops, bytes_accessed=held, transcendentals=0),
        compiler_params=pltpu.CompilerParams(vmem_limit_bytes=40 * 1024 * 1024),
        **kwargs,
    )(*args)


def shards(tokens, cotangent, expert_ids, node_groups, gate_weight, gate_proj, up_proj, down_proj):
    data_count = lax.axis_size("dp")
    group_count = lax.axis_size("group")
    node_count = lax.axis_size("node")
    tok_count, width = tokens.shape
    hid = down_proj.shape[1]
    per_group = expert_ids.shape[1] // node_groups.shape[1]
    family = group_count * tok_count
    capacity = (per_group * family + node_count - 1) // node_count
    count = node_count * capacity
    dot_flops = 2 * count * width * hid

    def shape(*dims):
        return jax.ShapeDtypeStruct(dims, BF16)

    def over(axis, blocks):
        return lax.all_to_all(blocks, axis, split_axis=0, concat_axis=0, tiled=True)

    (sent,) = run(
        functools.partial(send_kernel, node_count),
        (shape(group_count, tok_count, 2 * width + LANES),),
        tokens, cotangent, expert_ids.T, node_groups.T, gate_weight.T,
    )
    arrived = over("group", sent)
    slots, select = run(
        slot_kernel,
        (shape(node_count, capacity, 2 * width), shape(count, family)),
        arrived,
        flops=4 * count * family * width,
    )
    landed = over("node", slots).reshape(count, 2 * width)
    whole = pl.BlockSpec(memory_space=pltpu.VMEM)
    far = pl.BlockSpec(memory_space=pl.ANY)
    hidden, pair_grad, route_grad = run(
        expert_kernel,
        (shape(count, hid), shape(count, 2 * hid), shape(count, width)),
        landed, gate_proj[0], up_proj[0], down_proj[0],
        flops=5 * dot_flops,
        in_specs=[whole, far, far, far],
        out_specs=[whole] * 3,
        scratch_shapes=[
            pltpu.VMEM((width, hid), BF16),
            pltpu.VMEM((width, hid), BF16),
            pltpu.VMEM((hid, width), BF16),
            pltpu.SemaphoreType.DMA((3,)),
        ],
    )
    pair_grad, route_grad = lax.optimization_barrier((pair_grad, route_grad))
    returned = over("node", route_grad.reshape(node_count, capacity, width))

    def send_home(returned):
        group_grad = contract(select, returned.reshape(count, width), 0, 0).astype(BF16)
        return over("group", group_grad.reshape(group_count, tok_count, width))

    (partial,) = run(
        weights_kernel,
        (shape(data_count, width // data_count, 3 * hid),),
        landed, pair_grad, hidden,
        flops=3 * dot_flops,
    )
    total, home = to_owners(partial, returned, send_home)
    grad_tokens = jnp.sum(home.astype(F32), axis=0).astype(BF16)
    return (
        grad_tokens,
        total[None, :, :hid],
        total[None, :, hid : 2 * hid],
        total[:, 2 * hid :].T[None],
    )


def solution(mesh):
    rows = P(("dp", "group", "node"), None)
    experts = P(("group", "node"), None, None)
    return jax.shard_map(
        shards,
        mesh=mesh,
        in_specs=(rows,) * 5 + (experts,) * 3,
        out_specs=(
            rows,
            P(("group", "node"), "dp", None),
            P(("group", "node"), "dp", None),
            P(("group", "node"), None, "dp"),
        ),
        check_vma=False,
    )
```

```python
import functools

import jax
import jax.numpy as jnp
from jax import lax
from jax.experimental import pallas as pl
from jax.experimental.pallas import tpu as pltpu
from jax.sharding import PartitionSpec as P

F32 = jnp.float32
BF16 = jnp.bfloat16
LANES = 128


def contract(left, right, left_dim, right_dim):
    return lax.dot_general(
        left, right, (((left_dim,), (right_dim,)), ((), ())), preferred_element_type=F32
    )


def send_kernel(
    node_count, tokens_hbm, cot_hbm, ids_hbm, groups_hbm, gate_weight, sent, tokens, cotangent, expert_ids, node_groups, done
):
    loads = [
        pltpu.make_async_copy(ids_hbm, expert_ids, done.at[0]),
        pltpu.make_async_copy(groups_hbm, node_groups, done.at[1]),
        pltpu.make_async_copy(tokens_hbm, tokens, done.at[2]),
        pltpu.make_async_copy(cot_hbm, cotangent, done.at[3]),
    ]
    for load in loads:
        load.start()
    for load in loads:
        load.wait()
    group_count, tok_count, _ = sent.shape
    width = tokens.shape[1]
    choices, limit = expert_ids.shape[0], node_groups.shape[0]
    weights = gate_weight[...].astype(F32)
    expert = lax.broadcasted_iota(jnp.int32, (group_count * node_count, tok_count), 0)
    table = jnp.zeros(expert.shape, F32)
    for k in range(choices):
        table = table + jnp.where(expert_ids[k : k + 1, :] == expert, weights[k : k + 1, :], 0.0)
    for g in range(group_count):
        picked = node_groups[0:1, :] == g
        for j in range(1, limit):
            picked = picked | (node_groups[j : j + 1, :] == g)
        block = jnp.where(picked, table[g * node_count : (g + 1) * node_count, :], 0.0)
        sent[g, :, :width] = tokens[...]
        sent[g, :, width : 2 * width] = cotangent[...]
        sent[g, :, 2 * width :] = jnp.zeros((tok_count, LANES), BF16)
        sent[g, :node_count, 2 * width : 2 * width + tok_count] = block.astype(BF16)


def slot_kernel(arrived, slots_hbm, select, slots, done):
    group_count, tok_count, _ = arrived.shape
    node_count, capacity, width = slots.shape
    width = width // 2
    family = group_count * tok_count
    table = [arrived[g, :node_count, 2 * width : 2 * width + tok_count] for g in range(group_count)]
    table = jnp.concatenate([part.astype(F32) for part in table], axis=1)
    routed = table > 0
    row = lax.broadcasted_iota(jnp.int32, (family, family), 0)
    column = lax.broadcasted_iota(jnp.int32, (family, family), 1)
    earlier = jnp.where(row < column, 1.0, 0.0).astype(BF16)
    position = contract(jnp.where(routed, 1.0, 0.0).astype(BF16), earlier, 1, 0)
    place = jnp.where(routed, position, -1.0)[:, None, :]
    slot = lax.broadcasted_iota(jnp.int32, (node_count, capacity, family), 1).astype(F32)
    taken = place == slot
    picks = jnp.where(taken, 1.0, 0.0).reshape(node_count * capacity, family).astype(BF16)
    weighted = jnp.where(taken, table[:, None, :], 0.0).reshape(node_count * capacity, family).astype(BF16)
    select[...] = picks
    cut = width // 2
    stores = []
    for start in range(0, 2 * width, cut):
        part = slice(start, start + cut)
        block = arrived[:, :, part].reshape(family, cut)
        out = contract(picks if start < width else weighted, block, 1, 0)
        slots[:, :, part] = out.reshape(node_count, capacity, cut).astype(BF16)
        stores.append(pltpu.make_async_copy(slots.at[:, :, part], slots_hbm.at[:, :, part], done.at[len(stores)]))
        stores[-1].start()
    for store in stores:
        store.wait()


def expert_kernel(
    landed, gate_hbm, up_hbm, down_hbm, partial_hbm, pair_grad, gate_proj, up_proj, down_proj, partial, done, stored
):
    width, hid = gate_proj.shape
    count, cut, _ = partial.shape
    loads = [
        pltpu.make_async_copy(gate_hbm, gate_proj, done.at[0]),
        pltpu.make_async_copy(up_hbm, up_proj, done.at[1]),
        pltpu.make_async_copy(down_hbm, down_proj, done.at[2]),
    ]
    for load in loads:
        load.start()
    loads[0].wait()
    gate_value = contract(landed[:, :width], gate_proj[...], 1, 0)
    loads[1].wait()
    up_value = contract(landed[:, :width], up_proj[...], 1, 0)
    sigmoid = 1.0 / (1.0 + jnp.exp(-gate_value))
    silu = gate_value * sigmoid
    hidden = (silu * up_value).astype(BF16)
    loads[2].wait()
    hidden_grad = contract(landed[:, width:], down_proj[...], 1, 1)
    slope = up_value * sigmoid * (1.0 + gate_value * (1.0 - sigmoid))
    pair_grad[:, :hid] = (hidden_grad * slope).astype(BF16)
    pair_grad[:, hid:] = (hidden_grad * silu).astype(BF16)
    stores = []
    for block in range(count):
        rows = landed[:, block * cut : (block + 1) * cut]
        cot_rows = landed[:, width + block * cut : width + (block + 1) * cut]
        partial[block, :, : 2 * hid] = contract(rows, pair_grad[...], 0, 0).astype(BF16)
        partial[block, :, 2 * hid :] = contract(cot_rows, hidden, 0, 0).astype(BF16)
        stores.append(pltpu.make_async_copy(partial.at[block], partial_hbm.at[block], stored.at[block]))
        stores[-1].start()
    for store in stores:
        store.wait()


def route_kernel(pair_grad, gate_proj, up_proj, route_grad):
    width, hid = gate_proj.shape
    cut = width // 4
    for start in range(0, width, cut):
        part = slice(start, start + cut)
        grad = contract(pair_grad[:, :hid], gate_proj[part, :], 1, 1)
        grad = grad + contract(pair_grad[:, hid:], up_proj[part, :], 1, 1)
        route_grad[:, part] = grad.astype(BF16)


def run(kernel, out, *args, flops=0, **kwargs):
    held = sum(x.size * x.dtype.itemsize for x in (*args, *out))
    return pl.pallas_call(
        kernel,
        out_shape=out,
        cost_estimate=pl.CostEstimate(flops=flops, bytes_accessed=held, transcendentals=0),
        compiler_params=pltpu.CompilerParams(vmem_limit_bytes=40 * 1024 * 1024),
        **kwargs,
    )(*args)


def shards(tokens, cotangent, expert_ids, node_groups, gate_weight, gate_proj, up_proj, down_proj):
    data_count = lax.axis_size("dp")
    group_count = lax.axis_size("group")
    node_count = lax.axis_size("node")
    tok_count, width = tokens.shape
    hid = down_proj.shape[1]
    per_group = expert_ids.shape[1] // node_groups.shape[1]
    family = group_count * tok_count
    capacity = (per_group * family + node_count - 1) // node_count
    count = node_count * capacity
    dot_flops = 2 * count * width * hid

    def shape(*dims):
        return jax.ShapeDtypeStruct(dims, BF16)

    def over(axis, blocks):
        return lax.all_to_all(blocks, axis, split_axis=0, concat_axis=0, tiled=True)

    here = pl.BlockSpec(memory_space=pltpu.VMEM)
    far = pl.BlockSpec(memory_space=pltpu.HBM)
    (sent,) = run(
        functools.partial(send_kernel, node_count),
        (shape(group_count, tok_count, 2 * width + LANES),),
        tokens, cotangent, expert_ids.T, node_groups.T, gate_weight.T,
        in_specs=[far, far, far, far, here],
        out_specs=[here],
        scratch_shapes=[
            pltpu.VMEM((tok_count, width), BF16),
            pltpu.VMEM((tok_count, width), BF16),
            pltpu.VMEM(expert_ids.shape[::-1], jnp.int32),
            pltpu.VMEM(node_groups.shape[::-1], jnp.int32),
            pltpu.SemaphoreType.DMA((4,)),
        ],
    )
    arrived = over("group", sent)
    slots, select = run(
        slot_kernel,
        (shape(node_count, capacity, 2 * width), shape(count, family)),
        arrived,
        flops=4 * count * family * width,
        in_specs=[here],
        out_specs=[far, here],
        scratch_shapes=[pltpu.VMEM((node_count, capacity, 2 * width), BF16), pltpu.SemaphoreType.DMA((4,))],
    )
    landed = over("node", slots).reshape(count, 2 * width)
    partial, pair_grad = run(
        expert_kernel,
        (shape(data_count, width // data_count, 3 * hid), shape(count, 2 * hid)),
        landed, gate_proj[0], up_proj[0], down_proj[0],
        flops=6 * dot_flops,
        in_specs=[here, far, far, far],
        out_specs=[far, here],
        scratch_shapes=[
            pltpu.VMEM((width, hid), BF16),
            pltpu.VMEM((width, hid), BF16),
            pltpu.VMEM((hid, width), BF16),
            pltpu.VMEM((data_count, width // data_count, 3 * hid), BF16),
            pltpu.SemaphoreType.DMA((3,)),
            pltpu.SemaphoreType.DMA((data_count,)),
        ],
    )
    total = lax.psum_scatter(partial.reshape(width, 3 * hid), "dp", scatter_dimension=0, tiled=True)

    (route_grad,) = run(
        route_kernel, (shape(count, width),), pair_grad, gate_proj[0], up_proj[0], flops=2 * dot_flops
    )
    returned = over("node", route_grad.reshape(node_count, capacity, width))
    group_grad = contract(select, returned.reshape(count, width), 0, 0).astype(BF16)
    home = over("group", group_grad.reshape(group_count, tok_count, width))
    grad_tokens = jnp.sum(home.astype(F32), axis=0).astype(BF16)
    return (
        grad_tokens,
        total[None, :, :hid],
        total[None, :, hid : 2 * hid],
        total[:, 2 * hid :].T[None],
    )


def solution(mesh):
    rows = P(("dp", "group", "node"), None)
    experts = P(("group", "node"), None, None)
    return jax.shard_map(
        shards,
        mesh=mesh,
        in_specs=(rows,) * 5 + (experts,) * 3,
        out_specs=(
            rows,
            P(("group", "node"), "dp", None),
            P(("group", "node"), "dp", None),
            P(("group", "node"), None, "dp"),
        ),
        check_vma=False,
    )
```

```python
import functools

import jax
import jax.numpy as jnp
from jax import lax
from jax.experimental import pallas as pl
from jax.experimental.pallas import tpu as pltpu
from jax.sharding import PartitionSpec as P

F32 = jnp.float32
BF16 = jnp.bfloat16
LANES = 128
MIB = 1024 * 1024
ALONE = 63 * MIB


def contract(left, right, left_dim, right_dim):
    return lax.dot_general(
        left, right, (((left_dim,), (right_dim,)), ((), ())), preferred_element_type=F32
    )


def send_kernel(node_count, tokens, cotangent, expert_ids, node_groups, gate_weight, sent):
    group_count, tok_count, _ = sent.shape
    width = tokens.shape[1]
    choices, limit = expert_ids.shape[0], node_groups.shape[0]
    weights = gate_weight[...].astype(F32)
    expert = lax.broadcasted_iota(jnp.int32, (group_count * node_count, tok_count), 0)
    table = jnp.zeros(expert.shape, F32)
    for k in range(choices):
        table = table + jnp.where(expert_ids[k : k + 1, :] == expert, weights[k : k + 1, :], 0.0)
    for g in range(group_count):
        picked = node_groups[0:1, :] == g
        for j in range(1, limit):
            picked = picked | (node_groups[j : j + 1, :] == g)
        block = jnp.where(picked, table[g * node_count : (g + 1) * node_count, :], 0.0)
        sent[g, :, :width] = tokens[...]
        sent[g, :, width : 2 * width] = cotangent[...]
        sent[g, :, 2 * width :] = jnp.zeros((tok_count, LANES), BF16)
        sent[g, :node_count, 2 * width : 2 * width + tok_count] = block.astype(BF16)


def slot_kernel(arrived, slots, select):
    group_count, tok_count, _ = arrived.shape
    node_count, capacity, width = slots.shape
    width = width // 2
    family = group_count * tok_count
    table = [arrived[g, :node_count, 2 * width : 2 * width + tok_count] for g in range(group_count)]
    table = jnp.concatenate([part.astype(F32) for part in table], axis=1)
    routed = table > 0
    row = lax.broadcasted_iota(jnp.int32, (family, family), 0)
    column = lax.broadcasted_iota(jnp.int32, (family, family), 1)
    earlier = jnp.where(row < column, 1.0, 0.0).astype(BF16)
    position = contract(jnp.where(routed, 1.0, 0.0).astype(BF16), earlier, 1, 0)
    place = jnp.where(routed, position, -1.0)[:, None, :]
    slot = lax.broadcasted_iota(jnp.int32, (node_count, capacity, family), 1).astype(F32)
    taken = place == slot
    picks = jnp.where(taken, 1.0, 0.0).reshape(node_count * capacity, family).astype(BF16)
    weighted = jnp.where(taken, table[:, None, :], 0.0).reshape(node_count * capacity, family).astype(BF16)
    select[...] = picks
    cut = width // 2
    for start in range(0, 2 * width, cut):
        part = slice(start, start + cut)
        block = arrived[:, :, part].reshape(family, cut)
        out = contract(picks if start < width else weighted, block, 1, 0)
        slots[:, :, part] = out.reshape(node_count, capacity, cut).astype(BF16)


def expert_kernel(
    landed_hbm, gate_hbm, up_hbm, down_hbm, partial_hbm, pair_grad,
    landed, gate_proj, up_proj, down_proj, partial, done, stored,
):
    width, hid = gate_proj.shape
    count, cut, _ = partial.shape
    left, right = (slice(None), slice(0, width)), (slice(None), slice(width, 2 * width))
    loads = [
        pltpu.make_async_copy(landed_hbm.at[left], landed.at[left], done.at[0]),
        pltpu.make_async_copy(gate_hbm, gate_proj, done.at[1]),
        pltpu.make_async_copy(up_hbm, up_proj, done.at[2]),
        pltpu.make_async_copy(landed_hbm.at[right], landed.at[right], done.at[3]),
        pltpu.make_async_copy(down_hbm, down_proj, done.at[4]),
    ]
    for load in loads:
        load.start()
    loads[0].wait()
    loads[1].wait()
    gate_value = contract(landed[:, :width], gate_proj[...], 1, 0)
    loads[2].wait()
    up_value = contract(landed[:, :width], up_proj[...], 1, 0)
    sigmoid = 1.0 / (1.0 + jnp.exp(-gate_value))
    silu = gate_value * sigmoid
    hidden = (silu * up_value).astype(BF16)
    loads[3].wait()
    loads[4].wait()
    hidden_grad = contract(landed[:, width:], down_proj[...], 1, 1)
    slope = up_value * sigmoid * (1.0 + gate_value * (1.0 - sigmoid))
    pair_grad[:, :hid] = (hidden_grad * slope).astype(BF16)
    pair_grad[:, hid:] = (hidden_grad * silu).astype(BF16)
    stores = []
    for block in range(count):
        rows = landed[:, block * cut : (block + 1) * cut]
        cot_rows = landed[:, width + block * cut : width + (block + 1) * cut]
        partial[block, :, : 2 * hid] = contract(rows, pair_grad[...], 0, 0).astype(BF16)
        partial[block, :, 2 * hid :] = contract(cot_rows, hidden, 0, 0).astype(BF16)
        stores.append(pltpu.make_async_copy(partial.at[block], partial_hbm.at[block], stored.at[block]))
        stores[-1].start()
    for store in stores:
        store.wait()


def route_kernel(pair_grad, gate_proj, up_proj, route_grad):
    width, hid = gate_proj.shape
    cut = width // 4
    for start in range(0, width, cut):
        part = slice(start, start + cut)
        grad = contract(pair_grad[:, :hid], gate_proj[part, :], 1, 1)
        grad = grad + contract(pair_grad[:, hid:], up_proj[part, :], 1, 1)
        route_grad[:, part] = grad.astype(BF16)


def split_kernel(total, gate_out, up_out, down_out):
    hid = gate_out.shape[2]
    gate_out[0] = total[:, :hid]
    up_out[0] = total[:, hid : 2 * hid]
    down_out[0] = total[:, 2 * hid :].T


def run(kernel, out, *args, flops=0, vmem=40 * MIB, **kwargs):
    held = sum(x.size * x.dtype.itemsize for x in (*args, *out))
    return pl.pallas_call(
        kernel,
        out_shape=out,
        cost_estimate=pl.CostEstimate(flops=flops, bytes_accessed=held, transcendentals=0),
        compiler_params=pltpu.CompilerParams(vmem_limit_bytes=vmem),
        **kwargs,
    )(*args)


def shards(tokens, cotangent, expert_ids, node_groups, gate_weight, gate_proj, up_proj, down_proj):
    data_count = lax.axis_size("dp")
    group_count = lax.axis_size("group")
    node_count = lax.axis_size("node")
    tok_count, width = tokens.shape
    hid = down_proj.shape[1]
    per_group = expert_ids.shape[1] // node_groups.shape[1]
    family = group_count * tok_count
    capacity = (per_group * family + node_count - 1) // node_count
    count = node_count * capacity
    dot_flops = 2 * count * width * hid

    def shape(*dims):
        return jax.ShapeDtypeStruct(dims, BF16)

    def over(axis, blocks):
        return lax.all_to_all(blocks, axis, split_axis=0, concat_axis=0, tiled=True)

    here = pl.BlockSpec(memory_space=pltpu.VMEM)
    far = pl.BlockSpec(memory_space=pltpu.HBM)
    (sent,) = run(
        functools.partial(send_kernel, node_count),
        (shape(group_count, tok_count, 2 * width + LANES),),
        tokens, cotangent, expert_ids.T, node_groups.T, gate_weight.T,
        vmem=ALONE,
    )
    arrived = over("group", sent)
    slots, select = run(
        slot_kernel,
        (shape(node_count, capacity, 2 * width), shape(count, family)),
        arrived,
        flops=4 * count * family * width,
    )
    landed = over("node", slots).reshape(count, 2 * width)
    partial, pair_grad = run(
        expert_kernel,
        (shape(data_count, width // data_count, 3 * hid), shape(count, 2 * hid)),
        landed, gate_proj[0], up_proj[0], down_proj[0],
        flops=6 * dot_flops,
        vmem=ALONE,
        in_specs=[far] * 4,
        out_specs=[far, here],
        scratch_shapes=[
            pltpu.VMEM((count, 2 * width), BF16),
            pltpu.VMEM((width, hid), BF16),
            pltpu.VMEM((width, hid), BF16),
            pltpu.VMEM((hid, width), BF16),
            pltpu.VMEM((data_count, width // data_count, 3 * hid), BF16),
            pltpu.SemaphoreType.DMA((5,)),
            pltpu.SemaphoreType.DMA((data_count,)),
        ],
    )
    total = lax.psum_scatter(partial.reshape(width, 3 * hid), "dp", scatter_dimension=0, tiled=True)

    (route_grad,) = run(
        route_kernel, (shape(count, width),), pair_grad, gate_proj[0], up_proj[0], flops=2 * dot_flops
    )
    returned = over("node", route_grad.reshape(node_count, capacity, width))
    group_grad = contract(select, returned.reshape(count, width), 0, 0).astype(BF16)
    home = over("group", group_grad.reshape(group_count, tok_count, width))
    grad_tokens = jnp.sum(home.astype(F32), axis=0).astype(BF16)
    cut = width // data_count
    gate_out, up_out, down_out = run(
        split_kernel, (shape(1, cut, hid), shape(1, cut, hid), shape(1, hid, cut)), total, vmem=ALONE
    )
    return grad_tokens, gate_out, up_out, down_out


def solution(mesh):
    rows = P(("dp", "group", "node"), None)
    experts = P(("group", "node"), None, None)
    return jax.shard_map(
        shards,
        mesh=mesh,
        in_specs=(rows,) * 5 + (experts,) * 3,
        out_specs=(
            rows,
            P(("group", "node"), "dp", None),
            P(("group", "node"), "dp", None),
            P(("group", "node"), None, "dp"),
        ),
        check_vma=False,
    )
```

```python
import functools

import jax
import jax.numpy as jnp
from jax import lax
from jax.experimental import pallas as pl
from jax.experimental.pallas import tpu as pltpu
from jax.sharding import PartitionSpec as P

F32 = jnp.float32
BF16 = jnp.bfloat16
LANES = 128
MIB = 1024 * 1024
ALONE = 63 * MIB
BESIDE = 44 * MIB


def contract(left, right, left_dim, right_dim):
    return lax.dot_general(
        left, right, (((left_dim,), (right_dim,)), ((), ())), preferred_element_type=F32
    )


def send_kernel(node_count, tokens, cotangent, expert_ids, node_groups, gate_weight, sent):
    group_count, tok_count, _ = sent.shape
    width = tokens.shape[1]
    choices, limit = expert_ids.shape[0], node_groups.shape[0]
    weights = gate_weight[...].astype(F32)
    expert = lax.broadcasted_iota(jnp.int32, (group_count * node_count, tok_count), 0)
    table = jnp.zeros(expert.shape, F32)
    for k in range(choices):
        table = table + jnp.where(expert_ids[k : k + 1, :] == expert, weights[k : k + 1, :], 0.0)
    for g in range(group_count):
        picked = node_groups[0:1, :] == g
        for j in range(1, limit):
            picked = picked | (node_groups[j : j + 1, :] == g)
        block = jnp.where(picked, table[g * node_count : (g + 1) * node_count, :], 0.0)
        sent[g, :, :width] = tokens[...]
        sent[g, :, width : 2 * width] = cotangent[...]
        sent[g, :, 2 * width :] = jnp.zeros((tok_count, LANES), BF16)
        sent[g, :node_count, 2 * width : 2 * width + tok_count] = block.astype(BF16)


def slot_kernel(arrived, slots, select):
    group_count, tok_count, _ = arrived.shape
    node_count, capacity, width = slots.shape
    width = width // 2
    family = group_count * tok_count
    table = [arrived[g, :node_count, 2 * width : 2 * width + tok_count] for g in range(group_count)]
    table = jnp.concatenate([part.astype(F32) for part in table], axis=1)
    routed = table > 0
    row = lax.broadcasted_iota(jnp.int32, (family, family), 0)
    column = lax.broadcasted_iota(jnp.int32, (family, family), 1)
    earlier = jnp.where(row < column, 1.0, 0.0).astype(BF16)
    position = contract(jnp.where(routed, 1.0, 0.0).astype(BF16), earlier, 1, 0)
    place = jnp.where(routed, position, -1.0)[:, None, :]
    slot = lax.broadcasted_iota(jnp.int32, (node_count, capacity, family), 1).astype(F32)
    taken = place == slot
    picks = jnp.where(taken, 1.0, 0.0).reshape(node_count * capacity, family).astype(BF16)
    weighted = jnp.where(taken, table[:, None, :], 0.0).reshape(node_count * capacity, family).astype(BF16)
    select[...] = picks
    cut = width // 2
    for start in range(0, 2 * width, cut):
        part = slice(start, start + cut)
        block = arrived[:, :, part].reshape(family, cut)
        out = contract(picks if start < width else weighted, block, 1, 0)
        slots[:, :, part] = out.reshape(node_count, capacity, cut).astype(BF16)


def expert_kernel(
    landed, gate_proj, up_proj, down_proj, partial_hbm, pair_grad, partial, stored
):
    width, hid = gate_proj.shape
    count, cut, _ = partial.shape
    gate_value = contract(landed[:, :width], gate_proj[...], 1, 0)
    up_value = contract(landed[:, :width], up_proj[...], 1, 0)
    sigmoid = 1.0 / (1.0 + jnp.exp(-gate_value))
    silu = gate_value * sigmoid
    hidden = (silu * up_value).astype(BF16)
    hidden_grad = contract(landed[:, width:], down_proj[...], 1, 1)
    slope = up_value * sigmoid * (1.0 + gate_value * (1.0 - sigmoid))
    pair_grad[:, :hid] = (hidden_grad * slope).astype(BF16)
    pair_grad[:, hid:] = (hidden_grad * silu).astype(BF16)
    stores = []
    for block in range(count):
        rows = landed[:, block * cut : (block + 1) * cut]
        cot_rows = landed[:, width + block * cut : width + (block + 1) * cut]
        partial[block, :, : 2 * hid] = contract(rows, pair_grad[...], 0, 0).astype(BF16)
        partial[block, :, 2 * hid :] = contract(cot_rows, hidden, 0, 0).astype(BF16)
        stores.append(pltpu.make_async_copy(partial.at[block], partial_hbm.at[block], stored.at[block]))
        stores[-1].start()
    for store in stores:
        store.wait()


def route_kernel(pair_grad, gate_proj, up_proj, route_grad):
    width, hid = gate_proj.shape
    cut = width // 4
    for start in range(0, width, cut):
        part = slice(start, start + cut)
        grad = contract(pair_grad[:, :hid], gate_proj[part, :], 1, 1)
        grad = grad + contract(pair_grad[:, hid:], up_proj[part, :], 1, 1)
        route_grad[:, part] = grad.astype(BF16)


def split_kernel(total, gate_out, up_out, down_out):
    hid = gate_out.shape[2]
    gate_out[0] = total[:, :hid]
    up_out[0] = total[:, hid : 2 * hid]
    down_out[0] = total[:, 2 * hid :].T


def run(kernel, out, *args, flops=0, vmem=40 * MIB, **kwargs):
    held = sum(x.size * x.dtype.itemsize for x in (*args, *out))
    return pl.pallas_call(
        kernel,
        out_shape=out,
        cost_estimate=pl.CostEstimate(flops=flops, bytes_accessed=held, transcendentals=0),
        compiler_params=pltpu.CompilerParams(vmem_limit_bytes=vmem),
        **kwargs,
    )(*args)


def shards(tokens, cotangent, expert_ids, node_groups, gate_weight, gate_proj, up_proj, down_proj):
    data_count = lax.axis_size("dp")
    group_count = lax.axis_size("group")
    node_count = lax.axis_size("node")
    tok_count, width = tokens.shape
    hid = down_proj.shape[1]
    per_group = expert_ids.shape[1] // node_groups.shape[1]
    family = group_count * tok_count
    capacity = (per_group * family + node_count - 1) // node_count
    count = node_count * capacity
    dot_flops = 2 * count * width * hid

    def shape(*dims):
        return jax.ShapeDtypeStruct(dims, BF16)

    def over(axis, blocks):
        return lax.all_to_all(blocks, axis, split_axis=0, concat_axis=0, tiled=True)

    here = pl.BlockSpec(memory_space=pltpu.VMEM)
    far = pl.BlockSpec(memory_space=pltpu.HBM)
    (sent,) = run(
        functools.partial(send_kernel, node_count),
        (shape(group_count, tok_count, 2 * width + LANES),),
        tokens, cotangent, expert_ids.T, node_groups.T, gate_weight.T,
        vmem=ALONE,
    )
    arrived = over("group", sent)
    slots, select = run(
        slot_kernel,
        (shape(node_count, capacity, 2 * width), shape(count, family)),
        arrived,
        flops=4 * count * family * width,
    )
    landed = over("node", slots).reshape(count, 2 * width)
    partial, pair_grad = run(
        expert_kernel,
        (shape(data_count, width // data_count, 3 * hid), shape(count, 2 * hid)),
        landed, gate_proj[0], up_proj[0], down_proj[0],
        flops=6 * dot_flops,
        vmem=BESIDE,
        in_specs=[here] * 4,
        out_specs=[far, here],
        scratch_shapes=[
            pltpu.VMEM((data_count, width // data_count, 3 * hid), BF16),
            pltpu.SemaphoreType.DMA((data_count,)),
        ],
    )
    total = lax.psum_scatter(partial.reshape(width, 3 * hid), "dp", scatter_dimension=0, tiled=True)

    (route_grad,) = run(
        route_kernel, (shape(count, width),), pair_grad, gate_proj[0], up_proj[0], flops=2 * dot_flops
    )
    returned = over("node", route_grad.reshape(node_count, capacity, width))
    group_grad = contract(select, returned.reshape(count, width), 0, 0).astype(BF16)
    home = over("group", group_grad.reshape(group_count, tok_count, width))
    grad_tokens = jnp.sum(home.astype(F32), axis=0).astype(BF16)
    cut = width // data_count
    gate_out, up_out, down_out = run(
        split_kernel, (shape(1, cut, hid), shape(1, cut, hid), shape(1, hid, cut)), total, vmem=ALONE
    )
    return grad_tokens, gate_out, up_out, down_out


def solution(mesh):
    rows = P(("dp", "group", "node"), None)
    experts = P(("group", "node"), None, None)
    return jax.shard_map(
        shards,
        mesh=mesh,
        in_specs=(rows,) * 5 + (experts,) * 3,
        out_specs=(
            rows,
            P(("group", "node"), "dp", None),
            P(("group", "node"), "dp", None),
            P(("group", "node"), None, "dp"),
        ),
        check_vma=False,
    )
```

```python
import functools

import jax
import jax.numpy as jnp
from jax import lax
from jax.experimental import pallas as pl
from jax.experimental.pallas import tpu as pltpu
from jax.sharding import PartitionSpec as P

F32 = jnp.float32
BF16 = jnp.bfloat16
LANES = 128
MIB = 1024 * 1024
ALONE = 63 * MIB
BESIDE = 44 * MIB


def contract(left, right, left_dim, right_dim):
    return lax.dot_general(
        left, right, (((left_dim,), (right_dim,)), ((), ())), preferred_element_type=F32
    )


def send_kernel(node_count, tokens, cotangent, expert_ids, node_groups, gate_weight, sent):
    group_count, tok_count, _ = sent.shape
    width = tokens.shape[1]
    choices, limit = expert_ids.shape[0], node_groups.shape[0]
    weights = gate_weight[...].astype(F32)
    expert = lax.broadcasted_iota(jnp.int32, (group_count * node_count, tok_count), 0)
    table = jnp.zeros(expert.shape, F32)
    for k in range(choices):
        table = table + jnp.where(expert_ids[k : k + 1, :] == expert, weights[k : k + 1, :], 0.0)
    for g in range(group_count):
        picked = node_groups[0:1, :] == g
        for j in range(1, limit):
            picked = picked | (node_groups[j : j + 1, :] == g)
        block = jnp.where(picked, table[g * node_count : (g + 1) * node_count, :], 0.0)
        sent[g, :, :width] = tokens[...]
        sent[g, :, width : 2 * width] = cotangent[...]
        sent[g, :, 2 * width :] = jnp.zeros((tok_count, LANES), BF16)
        sent[g, :node_count, 2 * width : 2 * width + tok_count] = block.astype(BF16)


def slot_kernel(arrived, slots, select):
    group_count, tok_count, _ = arrived.shape
    node_count, capacity, width = slots.shape
    width = width // 2
    family = group_count * tok_count
    table = [arrived[g, :node_count, 2 * width : 2 * width + tok_count] for g in range(group_count)]
    table = jnp.concatenate([part.astype(F32) for part in table], axis=1)
    routed = table > 0
    row = lax.broadcasted_iota(jnp.int32, (family, family), 0)
    column = lax.broadcasted_iota(jnp.int32, (family, family), 1)
    earlier = jnp.where(row < column, 1.0, 0.0).astype(BF16)
    position = contract(jnp.where(routed, 1.0, 0.0).astype(BF16), earlier, 1, 0)
    place = jnp.where(routed, position, -1.0)[:, None, :]
    slot = lax.broadcasted_iota(jnp.int32, (node_count, capacity, family), 1).astype(F32)
    taken = place == slot
    picks = jnp.where(taken, 1.0, 0.0).reshape(node_count * capacity, family).astype(BF16)
    weighted = jnp.where(taken, table[:, None, :], 0.0).reshape(node_count * capacity, family).astype(BF16)
    select[...] = picks
    cut = width // 2
    for start in range(0, 2 * width, cut):
        part = slice(start, start + cut)
        block = arrived[:, :, part].reshape(family, cut)
        out = contract(picks if start < width else weighted, block, 1, 0)
        slots[:, :, part] = out.reshape(node_count, capacity, cut).astype(BF16)


def expert_kernel(
    landed, gate_proj, up_proj, down_proj, partial_hbm, pair_grad, partial, stored
):
    width, hid = gate_proj.shape
    count, cut, _ = partial.shape
    gate_value = contract(landed[:, :width], gate_proj[...], 1, 0)
    up_value = contract(landed[:, :width], up_proj[...], 1, 0)
    sigmoid = 1.0 / (1.0 + jnp.exp(-gate_value))
    silu = gate_value * sigmoid
    hidden = (silu * up_value).astype(BF16)
    hidden_grad = contract(landed[:, width:], down_proj[...], 1, 1)
    slope = up_value * sigmoid * (1.0 + gate_value * (1.0 - sigmoid))
    pair_grad[:, :hid] = (hidden_grad * slope).astype(BF16)
    pair_grad[:, hid:] = (hidden_grad * silu).astype(BF16)
    stores = []
    for block in range(count):
        rows = landed[:, block * cut : (block + 1) * cut]
        cot_rows = landed[:, width + block * cut : width + (block + 1) * cut]
        partial[block, :, : 2 * hid] = contract(rows, pair_grad[...], 0, 0).astype(BF16)
        partial[block, :, 2 * hid :] = contract(cot_rows, hidden, 0, 0).astype(BF16)
        stores.append(pltpu.make_async_copy(partial.at[block], partial_hbm.at[block], stored.at[block]))
        stores[-1].start()
    for store in stores:
        store.wait()


def route_kernel(pair_grad, gate_proj, up_proj, route_grad):
    width, hid = gate_proj.shape
    cut = width // 4
    for start in range(0, width, cut):
        part = slice(start, start + cut)
        grad = contract(pair_grad[:, :hid], gate_proj[part, :], 1, 1)
        grad = grad + contract(pair_grad[:, hid:], up_proj[part, :], 1, 1)
        route_grad[:, part] = grad.astype(BF16)


def split_kernel(total, gate_out, up_out, down_out):
    hid = gate_out.shape[2]
    gate_out[0] = total[:, :hid]
    up_out[0] = total[:, hid : 2 * hid]
    down_out[0] = total[:, 2 * hid :].T


def run(kernel, out, *args, flops=0, vmem=40 * MIB, **kwargs):
    held = sum(x.size * x.dtype.itemsize for x in (*args, *out))
    return pl.pallas_call(
        kernel,
        out_shape=out,
        cost_estimate=pl.CostEstimate(flops=flops, bytes_accessed=held, transcendentals=0),
        compiler_params=pltpu.CompilerParams(vmem_limit_bytes=vmem),
        **kwargs,
    )(*args)


def shards(tokens, cotangent, expert_ids, node_groups, gate_weight, gate_proj, up_proj, down_proj):
    data_count = lax.axis_size("dp")
    group_count = lax.axis_size("group")
    node_count = lax.axis_size("node")
    tok_count, width = tokens.shape
    hid = down_proj.shape[1]
    per_group = expert_ids.shape[1] // node_groups.shape[1]
    family = group_count * tok_count
    capacity = (per_group * family + node_count - 1) // node_count
    count = node_count * capacity
    dot_flops = 2 * count * width * hid

    def shape(*dims):
        return jax.ShapeDtypeStruct(dims, BF16)

    def over(axis, blocks):
        return lax.all_to_all(blocks, axis, split_axis=0, concat_axis=0, tiled=True)

    here = pl.BlockSpec(memory_space=pltpu.VMEM)
    far = pl.BlockSpec(memory_space=pltpu.HBM)
    (sent,) = run(
        functools.partial(send_kernel, node_count),
        (shape(group_count, tok_count, 2 * width + LANES),),
        tokens, cotangent, expert_ids.T, node_groups.T, gate_weight.T,
        vmem=ALONE,
    )
    arrived = over("group", sent)
    slots, select = run(
        slot_kernel,
        (shape(node_count, capacity, 2 * width), shape(count, family)),
        arrived,
        flops=4 * count * family * width,
    )
    landed = over("node", slots).reshape(count, 2 * width)
    partial, pair_grad = run(
        expert_kernel,
        (shape(data_count, width // data_count, 3 * hid), shape(count, 2 * hid)),
        landed, gate_proj[0], up_proj[0], down_proj[0],
        flops=6 * dot_flops,
        vmem=BESIDE,
        in_specs=[here] * 4,
        out_specs=[far, here],
        scratch_shapes=[
            pltpu.VMEM((data_count, width // data_count, 3 * hid), BF16),
            pltpu.SemaphoreType.DMA((data_count,)),
        ],
    )
    total = lax.psum_scatter(partial.reshape(width, 3 * hid), "dp", scatter_dimension=0, tiled=True)

    (route_grad,) = run(
        route_kernel, (shape(count, width),), pair_grad, gate_proj[0], up_proj[0], flops=2 * dot_flops
    )
    returned = over("node", route_grad.reshape(node_count, capacity, width))
    group_grad = contract(select, returned.reshape(count, width), 0, 0).astype(BF16)
    home = over("group", group_grad.reshape(group_count, tok_count, width))
    grad_tokens = jnp.sum(home.astype(F32), axis=0).astype(BF16)
    cut = width // data_count
    step = cut // 2
    gate_out, up_out, down_out = run(
        split_kernel,
        (shape(1, cut, hid), shape(1, cut, hid), shape(1, hid, cut)),
        total,
        vmem=ALONE,
        grid=(2,),
        in_specs=[pl.BlockSpec((step, 3 * hid), lambda i: (i, 0))],
        out_specs=[
            pl.BlockSpec((1, step, hid), lambda i: (0, i, 0)),
            pl.BlockSpec((1, step, hid), lambda i: (0, i, 0)),
            pl.BlockSpec((1, hid, step), lambda i: (0, 0, i)),
        ],
    )
    return grad_tokens, gate_out, up_out, down_out


def solution(mesh):
    rows = P(("dp", "group", "node"), None)
    experts = P(("group", "node"), None, None)
    return jax.shard_map(
        shards,
        mesh=mesh,
        in_specs=(rows,) * 5 + (experts,) * 3,
        out_specs=(
            rows,
            P(("group", "node"), "dp", None),
            P(("group", "node"), "dp", None),
            P(("group", "node"), None, "dp"),
        ),
        check_vma=False,
    )
```
